32 devices in a mesh: pipe: 4 (over x, core), dp: 2 (over y), tensor: 4 (over z).
Axes of the slice: x: 2, y: 2, z: 4, core: 2. Of those that a mesh axis runs over, the one named last changes fastest.
Arguments:
- section_inputs: bfloat16 [4, 1024, 4096], P('pipe', ('dp', 'tensor')), may hold values from -36 to 36
- norm_gain: bfloat16 [4, 4096], P('pipe'), may hold values from 0.5 to 1.5
- query_weight: bfloat16 [4, 4096, 4096], P('pipe', None, 'tensor'), may hold values from -0.09375 to 0.09375
- key_weight: bfloat16 [4, 4096, 512], P('pipe', None, 'tensor'), may hold values from -0.09375 to 0.09375
- value_weight: bfloat16 [4, 4096, 512], P('pipe', None, 'tensor'), may hold values from -0.09375 to 0.09375
- output_weight: bfloat16 [4, 4096, 4096], P('pipe', 'tensor'), may hold values from -0.09375 to 0.09375
- upstream_grad: bfloat16 [1024, 4096], P(('dp', 'tensor')), may hold values from -6 to 6
- document_ids: int32 [2, 512], P('dp'), may hold values from 0 to 3, never falling along the last dimension, each value on 1 to 256 neighbouring positions
Outputs:
- input_grads: bfloat16 [4, 1024, 4096], P('pipe', ('dp', 'tensor'))
- query_grads: float32 [4, 4096, 4096], P('pipe', 'dp', 'tensor')
- key_grads: float32 [4, 4096, 512], P('pipe', 'dp', 'tensor')
- value_grads: float32 [4, 4096, 512], P('pipe', 'dp', 'tensor')
- output_grads: float32 [4, 4096, 4096], P('pipe', 'tensor', 'dp')
The draws below stay inside these ranges and needn't reach their ends.
Inputs may be any that keep to these rules, and one draw needn't show every extreme that they name: `document_ids`: along each sequence the document numbers never fall; each of the 4 documents holds 1 to 256 tokens, one of them exactly 256.
All inputs are finite; a program needn't handle non-finite values.
Results may differ from the reference program's by a relative error of at most 0.03.
Values may be sent and summed in bfloat16 or wider, within the bound.
A program may use at most 256 MiB of HBM per device.

```python
import math
import jax
import jax.numpy as jnp
import numpy as np
from jax import lax

D = 4096
HEADS = 32
KV = 4
HD = 128
DOCS = 4
SEQ = 512
TOKENS = 1024
QW = 4096
KVW = 512
N_PIPE = 4
N_DP = 2
N_TENSOR = 4


def draw_section_inputs(key, part):
    first, second, third = jax.random.split(key, 3)
    shape = (N_PIPE, TOKENS, D)
    base = jnp.clip(jax.random.normal(first, shape, jnp.float32), -4.0, 4.0)
    row_scale = jnp.exp(jax.random.uniform(second, (N_PIPE, TOKENS, 1), jnp.float32, math.log(0.3), math.log(3.0)))
    col_scale = jnp.exp(jax.random.uniform(third, (N_PIPE, 1, D), jnp.float32, math.log(0.3), math.log(3.0)))
    return (base * row_scale * col_scale).astype(jnp.bfloat16)


def block_scale(key, dims, cuts, low, top_value):
    loudness, own = 1.0, jax.random.fold_in(key, 6)
    for axis_at, parts in cuts:
        draws = jnp.exp(jax.random.uniform(jax.random.fold_in(own, axis_at), (parts,), jnp.float32, low / len(cuts), top_value / len(cuts)))
        loudness = loudness * jnp.repeat(draws, dims[axis_at] // parts).reshape([-1 if axis == axis_at else 1 for axis in range(len(dims))])
    return loudness


def profile(count, total, most, skew):
    portions = [(1 << 20) // math.isqrt(grade ** skew) + 1 for grade in range(2, count + 1)]
    spare, counts = total - most - (count - 1), [1] * (count - 1)
    while spare > 0:
        candidates = [i for i in range(count - 1) if counts[i] < most]
        mass, remaining = sum([portions[i] for i in candidates]), spare
        for i in candidates:
            more = min(most - counts[i], max(1, remaining * portions[i] // mass), spare)
            counts[i] = counts[i] + more
            spare = spare - more
    return np.array([most] + counts)


def ragged(rng, count, total, limit, skew):
    if count == 2:
        one = jax.random.randint(rng, (), max(1, total - limit), min(limit, total - 1) + 1)
        return jnp.stack([one, total - one])
    tallies = jnp.asarray(profile(count, total, limit, skew), jnp.int32)
    pairs = (count - 1) // 2
    source_of, sink = tallies[1:1 + 2 * pairs:2], tallies[2:2 + 2 * pairs:2]
    room = jnp.minimum(source_of - 1, limit - sink)
    moved = jax.random.randint(jax.random.fold_in(rng, 1), (pairs,), 0, 1 << 20) % (room + 1)
    tallies = tallies.at[1:1 + 2 * pairs:2].set(source_of - moved).at[2:2 + 2 * pairs:2].set(sink + moved)
    return tallies[jax.random.permutation(jax.random.fold_in(rng, 2), count)]


def noise(own_key, extent, deviation, reach, shards=(), kind=jnp.bfloat16):
    values = jax.random.normal(own_key, extent, jnp.float32) * deviation
    if len(shards) > 0:
        values = block_scale(own_key, extent, shards, -0.22, 0.18) * values
    return jnp.clip(values, min=-reach, max=reach).astype(kind)


def setup_inputs(seed: int = 0) -> dict:
    arg_keys = jax.random.split(jax.random.key(seed), 9)
    return {
        "section_inputs": draw_section_inputs(jax.random.fold_in(arg_keys[8], 71), 0),
        "norm_gain": jnp.clip(1.0 + 0.1 * jax.random.normal(arg_keys[1], (N_PIPE, D), jnp.float32), 0.5, 1.5).astype(jnp.bfloat16),
        "query_weight": noise(arg_keys[2], (N_PIPE, D, QW), D ** -0.5, 0.09375, ((0, 4), (2, 4))),
        "key_weight": noise(arg_keys[3], (N_PIPE, D, KVW), D ** -0.5, 0.09375, ((0, 4), (2, 4))),
        "value_weight": noise(arg_keys[4], (N_PIPE, D, KVW), D ** -0.5, 0.09375, ((0, 4), (2, 4))),
        "output_weight": noise(arg_keys[5], (N_PIPE, QW, D), QW ** -0.5, 0.09375, ((0, 4), (1, 4))),
        "upstream_grad": noise(arg_keys[6], (TOKENS, D), 1.0, 6.0, ((0, 8),)),
        "document_ids": jax.vmap(lambda own: jnp.searchsorted(jnp.cumsum(ragged(own, DOCS, SEQ, SEQ // 2, 0)), jnp.arange(SEQ), side="right"))(jax.random.split(arg_keys[7], N_DP)).reshape((N_DP, SEQ)).astype(jnp.int32),
    }


epsilon = 1e-05
rope_base = 500000.0

def to_low(values):
    return lax.optimization_barrier(values.astype(jnp.bfloat16))

def position_tables(document_ids, head_dim):
    seq_len = document_ids.shape[1]
    index = jnp.arange(seq_len, dtype=jnp.int32)
    earlier = (document_ids[:, None, :] < document_ids[:, :, None]).astype(jnp.int32)
    position = index[None, :] - lax.optimization_barrier(jnp.sum(earlier, axis=2)).astype(jnp.int32)
    half = head_dim // 2
    expo = jnp.arange(half, dtype=jnp.float32) * (2.0 / head_dim)
    freq = jnp.exp(expo * -math.log(rope_base))
    angle = position.astype(jnp.float32)[:, :, None] * freq
    same = document_ids[:, :, None] == document_ids[:, None, :]
    causal = index[:, None] >= index[None, :]
    visible = jnp.logical_and(same, causal[None])
    return (jnp.cos(angle), jnp.sin(angle), visible)

def rotate(vector, rot_cos, rot_sin, direction):
    half = vector.shape[-1] // 2
    first = vector[..., :half]
    second = vector[..., half:]
    return jnp.concatenate([first * rot_cos - direction * second * rot_sin, second * rot_cos + direction * first * rot_sin], axis=-1)

def normalize(rows, gain):
    values = rows.astype(jnp.float32)
    inverse = lax.rsqrt(lax.optimization_barrier(jnp.mean(values * values, axis=-1, keepdims=True)) + epsilon)
    unit_rows = values * inverse
    normed = (unit_rows * gain.astype(jnp.float32)).astype(jnp.bfloat16)
    return (inverse, unit_rows, normed)

def attention_forward(query_rot, key_rot, value_low, visible):
    scale = 1.0 / math.sqrt(HD)
    scores = jnp.einsum('bqngd,bknd->bngqk', query_rot.astype(jnp.float32), key_rot.astype(jnp.float32)) * scale
    expo = jnp.where(visible[:, None, None], jnp.exp(scores), 0.0)
    prob = expo / lax.optimization_barrier(jnp.sum(expo, axis=-1, keepdims=True))
    prob_low = to_low(prob)
    mixed = jnp.einsum('bngqk,bknd->bqngd', prob_low.astype(jnp.float32), value_low.astype(jnp.float32))
    return (prob, prob_low, to_low(mixed))

def attention_backward(grad_mixed, query_rot, key_rot, value_low, prob, prob_low, rot_cos, rot_sin):
    scale = 1.0 / math.sqrt(HD)
    grad_float = grad_mixed.astype(jnp.float32)
    grad_value = jnp.einsum('bngqk,bqngd->bknd', prob_low.astype(jnp.float32), grad_float)
    grad_prob = jnp.einsum('bqngd,bknd->bngqk', grad_float, value_low.astype(jnp.float32))
    grad_score = prob * (grad_prob - lax.optimization_barrier(jnp.sum(grad_prob * prob, axis=-1, keepdims=True))) * scale
    score_low = to_low(grad_score).astype(jnp.float32)
    grad_query = jnp.einsum('bngqk,bknd->bqngd', score_low, key_rot.astype(jnp.float32))
    grad_key = jnp.einsum('bngqk,bqngd->bknd', score_low, query_rot.astype(jnp.float32))
    grad_query = rotate(grad_query, rot_cos[:, :, None, None, :], rot_sin[:, :, None, None, :], -1.0)
    grad_key = rotate(grad_key, rot_cos[:, :, None, :], rot_sin[:, :, None, :], -1.0)
    return (to_low(grad_query), to_low(grad_key), to_low(grad_value))

def back_norm(grad_normed, unit_rows, inverse, gain, incoming):
    grad_unit = grad_normed * gain.astype(jnp.float32)
    branch = (grad_unit - unit_rows * lax.optimization_barrier(jnp.mean(grad_unit * unit_rows, axis=-1, keepdims=True))) * inverse
    return (incoming.astype(jnp.float32) + branch).astype(jnp.bfloat16)

def group_sum(left, right):

    def step(total, pair):
        part = jnp.dot(pair[0].T, pair[1], preferred_element_type=jnp.float32)
        rounded = lax.optimization_barrier(part.astype(jnp.bfloat16))
        return (total + rounded.astype(jnp.float32), None)
    start = jnp.zeros((left.shape[2], right.shape[2]), jnp.float32)
    total, unused = lax.scan(step, start, (left, right))
    return total

def head_block_sum(flat_query, flat_key, flat_value, w_query, w_key, w_value):
    q_block = QW // N_TENSOR
    k_block = KVW // N_TENSOR
    total = jnp.zeros((flat_query.shape[0], D), jnp.float32)
    for block in range(N_TENSOR):
        qs = slice(block * q_block, (block + 1) * q_block)
        ks = slice(block * k_block, (block + 1) * k_block)
        partial_value = jnp.dot(flat_query[:, qs], w_query[:, qs].T, preferred_element_type=jnp.float32) + jnp.dot(flat_key[:, ks], w_key[:, ks].T, preferred_element_type=jnp.float32) + jnp.dot(flat_value[:, ks], w_value[:, ks].T, preferred_element_type=jnp.float32)
        total = total + to_low(partial_value).astype(jnp.float32)
    return total

def reference(section_inputs, norm_gain, query_weight, key_weight, value_weight, output_weight, upstream_grad, document_ids):
    groups = document_ids.shape[0]
    seq_len = document_ids.shape[1]
    group = HEADS // KV
    rot_cos, rot_sin, visible = position_tables(document_ids, HD)
    scale_out = 1.0 / math.sqrt(groups * seq_len)
    cotangent = upstream_grad.reshape(groups, seq_len, D)
    input_list = []
    query_list = []
    key_list = []
    value_list = []
    output_list = []
    for section in range(N_PIPE - 1, -1, -1):
        rows = section_inputs[section].reshape(groups, seq_len, D)
        gain = norm_gain[section]
        inverse, unit_rows, normed = normalize(rows, gain)
        flat = normed.reshape(groups * seq_len, D)
        query = jnp.dot(flat, query_weight[section], preferred_element_type=jnp.float32).reshape(groups, seq_len, KV, group, HD)
        keys = jnp.dot(flat, key_weight[section], preferred_element_type=jnp.float32).reshape(groups, seq_len, KV, HD)
        values = jnp.dot(flat, value_weight[section], preferred_element_type=jnp.float32).reshape(groups, seq_len, KV, HD)
        query_rot = to_low(rotate(query, rot_cos[:, :, None, None, :], rot_sin[:, :, None, None, :], 1.0))
        key_rot = to_low(rotate(keys, rot_cos[:, :, None, :], rot_sin[:, :, None, :], 1.0))
        value_low = to_low(values)
        prob, prob_low, mixed = attention_forward(query_rot, key_rot, value_low, visible)
        grad_mixed = to_low(jnp.dot(cotangent.reshape(groups * seq_len, D), output_weight[section].T, preferred_element_type=jnp.float32))
        grad_query, grad_key, grad_value = attention_backward(grad_mixed.reshape(groups, seq_len, KV, group, HD), query_rot, key_rot, value_low, prob, prob_low, rot_cos, rot_sin)
        flat_query = grad_query.reshape(groups * seq_len, QW)
        flat_key = grad_key.reshape(groups * seq_len, KVW)
        flat_value = grad_value.reshape(groups * seq_len, KVW)
        grad_normed = head_block_sum(flat_query, flat_key, flat_value, query_weight[section], key_weight[section], value_weight[section])
        result = back_norm(grad_normed.reshape(groups, seq_len, D), unit_rows, inverse, gain, cotangent)
        query_list.append(group_sum(normed, flat_query.reshape(groups, seq_len, QW)) * scale_out)
        key_list.append(group_sum(normed, flat_key.reshape(groups, seq_len, KVW)) * scale_out)
        value_list.append(group_sum(normed, flat_value.reshape(groups, seq_len, KVW)) * scale_out)
        output_list.append(group_sum(mixed.reshape(groups, seq_len, QW), cotangent) * scale_out)
        input_list.append(result.reshape(groups * seq_len, D))
        cotangent = result
    input_grads = jnp.stack(input_list[::-1])
    query_grads = jnp.stack(query_list[::-1])
    key_grads = jnp.stack(key_list[::-1])
    value_grads = jnp.stack(value_list[::-1])
    output_grads = jnp.stack(output_list[::-1])
    return (input_grads, query_grads, key_grads, value_grads, output_grads)
```

```python
import functools
import math

import jax
import jax.numpy as jnp
from jax import lax
from jax.experimental import pallas as pl
from jax.experimental.pallas import tpu as pltpu
from jax.sharding import PartitionSpec as P

HD = 128

epsilon = 1e-05
rope_base = 500000.0


def position_tables(document_ids, head_dim):
    ids = document_ids[0]
    index = jnp.arange(ids.shape[0], dtype=jnp.int32)
    earlier = (ids[None, :] < ids[:, None]).astype(jnp.int32)
    position = index - jnp.sum(earlier, axis=1)
    half = head_dim // 2
    expo = jnp.arange(half, dtype=jnp.float32) * (2.0 / head_dim)
    freq = jnp.exp(expo * -math.log(rope_base))
    angle = position.astype(jnp.float32)[:, None] * freq
    cos, sin = jnp.cos(angle), jnp.sin(angle)
    same = ids[:, None] == ids[None, :]
    visible = jnp.logical_and(same, index[:, None] >= index[None, :])
    return (
        jnp.concatenate([cos, cos], axis=1),
        jnp.concatenate([-sin, sin], axis=1),
        visible.astype(jnp.float32),
    )


def normalize(rows, gain):
    values = rows.astype(jnp.float32)
    inverse = lax.rsqrt(jnp.mean(values * values, axis=-1, keepdims=True) + epsilon)
    unit_rows = values * inverse
    normed = (unit_rows * gain.astype(jnp.float32)).astype(jnp.bfloat16)
    return (inverse, unit_rows, normed)


def back_norm(grad_normed, unit_rows, inverse, gain, incoming):
    grad_unit = grad_normed * gain.astype(jnp.float32)
    branch = (
        grad_unit - unit_rows * jnp.mean(grad_unit * unit_rows, axis=-1, keepdims=True)
    ) * inverse
    return (incoming.astype(jnp.float32) + branch).astype(jnp.bfloat16)


def dot_nt(left, right):
    return lax.dot_general(
        left, right, (((1,), (1,)), ((), ())), preferred_element_type=jnp.float32
    )


def dot_tn(left, right):
    return lax.dot_general(
        left, right, (((0,), (0,)), ((), ())), preferred_element_type=jnp.float32
    )


def forward_kernel(group, q_ref, k_ref, v_ref, cos_ref, sin_ref, vis_ref,
                   qr_ref, kr_ref, vl_ref, prob_ref, mixed_ref):
    def turned(vector):
        return vector * cos_ref[...] + pltpu.roll(vector, HD // 2, 1) * sin_ref[...]

    @pl.when(lax.rem(pl.program_id(0), group) == 0)
    def _():
        kr_ref[...] = turned(k_ref[...]).astype(jnp.bfloat16)
        vl_ref[...] = v_ref[...].astype(jnp.bfloat16)

    query = turned(q_ref[...]).astype(jnp.bfloat16)
    qr_ref[...] = query
    scores = dot_nt(query, kr_ref[...]) * (1.0 / math.sqrt(HD))
    expo = jnp.where(vis_ref[...] > 0.0, jnp.exp(scores), 0.0)
    prob = (expo / jnp.sum(expo, axis=-1, keepdims=True)).astype(jnp.bfloat16)
    prob_ref[0] = prob
    mixed_ref[...] = jnp.dot(prob, vl_ref[...], preferred_element_type=jnp.float32).astype(
        jnp.bfloat16
    )


def attention_forward(query, keys, values, cos, sin, visible):
    seq, q_width = query.shape
    k_width = keys.shape[1]
    heads, group = q_width // HD, q_width // k_width
    per_head = pl.BlockSpec((seq, HD), lambda h: (0, h))
    per_kv = pl.BlockSpec((seq, HD), lambda h: (0, h // group))
    table = pl.BlockSpec((seq, HD), lambda h: (0, 0))
    square = pl.BlockSpec((seq, seq), lambda h: (0, 0))
    return pl.pallas_call(
        functools.partial(forward_kernel, group),
        grid=(heads,),
        in_specs=[per_head, per_kv, per_kv, table, table, square],
        out_specs=[
            per_head,
            per_kv,
            per_kv,
            pl.BlockSpec((1, seq, seq), lambda h: (h, 0, 0)),
            per_head,
        ],
        out_shape=[
            jax.ShapeDtypeStruct((seq, q_width), jnp.bfloat16),
            jax.ShapeDtypeStruct((seq, k_width), jnp.bfloat16),
            jax.ShapeDtypeStruct((seq, k_width), jnp.bfloat16),
            jax.ShapeDtypeStruct((heads, seq, seq), jnp.bfloat16),
            jax.ShapeDtypeStruct((seq, q_width), jnp.bfloat16),
        ],
        compiler_params=pltpu.CompilerParams(vmem_limit_bytes=32 * 1024 * 1024),
        cost_estimate=pl.CostEstimate(
            flops=4 * heads * seq * seq * HD,
            bytes_accessed=2 * heads * seq * seq + 8 * seq * q_width,
            transcendentals=heads * seq * seq,
        ),
    )(query, keys, values, cos, sin, visible)


def backward_kernel(group, gm_ref, q_ref, k_ref, v_ref, prob_ref, cos_ref, sin_ref,
                    gq_ref, gk_ref, gv_ref, key_total, value_total):
    member = lax.rem(pl.program_id(0), group)

    def turned_back(vector):
        return vector * cos_ref[...] - pltpu.roll(vector, HD // 2, 1) * sin_ref[...]

    @pl.when(member == 0)
    def _():
        key_total[...] = jnp.zeros_like(key_total)
        value_total[...] = jnp.zeros_like(value_total)

    grad_mixed = gm_ref[...]
    prob_low = prob_ref[0]
    value_total[...] += dot_tn(prob_low, grad_mixed)
    grad_prob = dot_nt(grad_mixed, v_ref[...])
    prob = prob_low.astype(jnp.float32)
    inner = jnp.sum(grad_prob * prob, axis=-1, keepdims=True)
    score_low = (prob * (grad_prob - inner) * (1.0 / math.sqrt(HD))).astype(jnp.bfloat16)
    gq_ref[...] = turned_back(
        jnp.dot(score_low, k_ref[...], preferred_element_type=jnp.float32)
    ).astype(jnp.bfloat16)
    key_total[...] += dot_tn(score_low, q_ref[...])

    @pl.when(member == group - 1)
    def _():
        gk_ref[...] = turned_back(key_total[...]).astype(jnp.bfloat16)
        gv_ref[...] = value_total[...].astype(jnp.bfloat16)


def attention_backward(grad_mixed, query_rot, key_rot, value_low, prob_low, cos, sin):
    seq, q_width = query_rot.shape
    k_width = key_rot.shape[1]
    heads, group = q_width // HD, q_width // k_width
    per_head = pl.BlockSpec((seq, HD), lambda h: (0, h))
    per_kv = pl.BlockSpec((seq, HD), lambda h: (0, h // group))
    table = pl.BlockSpec((seq, HD), lambda h: (0, 0))
    return pl.pallas_call(
        functools.partial(backward_kernel, group),
        grid=(heads,),
        in_specs=[
            per_head,
            per_head,
            per_kv,
            per_kv,
            pl.BlockSpec((1, seq, seq), lambda h: (h, 0, 0)),
            table,
            table,
        ],
        out_specs=[per_head, per_kv, per_kv],
        out_shape=[
            jax.ShapeDtypeStruct((seq, q_width), jnp.bfloat16),
            jax.ShapeDtypeStruct((seq, k_width), jnp.bfloat16),
            jax.ShapeDtypeStruct((seq, k_width), jnp.bfloat16),
        ],
        scratch_shapes=[pltpu.VMEM((seq, HD), jnp.float32)] * 2,
        compiler_params=pltpu.CompilerParams(vmem_limit_bytes=32 * 1024 * 1024),
        cost_estimate=pl.CostEstimate(
            flops=10 * heads * seq * seq * HD,
            bytes_accessed=2 * heads * seq * seq + 6 * seq * q_width,
            transcendentals=0,
        ),
    )(grad_mixed, query_rot, key_rot, value_low, prob_low, cos, sin)


def local(
    section_inputs,
    norm_gain,
    query_weight,
    key_weight,
    value_weight,
    output_weight,
    upstream_grad,
    document_ids,
):
    pipes = lax.axis_size("pipe")
    groups = lax.axis_size("dp")
    ranks = lax.axis_size("tensor")
    section = lax.axis_index("pipe")
    sequence = lax.axis_index("dp")
    rank = lax.axis_index("tensor")
    width = section_inputs.shape[2]
    seq_len = document_ids.shape[1]
    rows = seq_len // ranks
    part = width // groups
    gain = norm_gain[0]
    w_query, w_key, w_value, w_output = (
        query_weight[0],
        key_weight[0],
        value_weight[0],
        output_weight[0],
    )
    last = pipes - 1

    def relay(block, source, target, by):
        pairs = [
            (source * ranks + i, target * ranks + (i + by) % ranks) for i in range(ranks)
        ]
        return lax.ppermute(block, ("pipe", "tensor"), pairs)

    def swap(block, by):
        return lax.ppermute(block, "dp", [(i, (i + by) % groups) for i in range(groups)])

    def columns_of(array, by):
        at = lax.rem(sequence + by, groups) * part
        return lax.dynamic_slice_in_dim(array, at, part, axis=1)

    def every_sequence(array):
        return jnp.concatenate([array] + [swap(array, by) for by in range(1, groups)], axis=0)

    def every_sequence_part(array):
        return jnp.concatenate(
            [columns_of(array, 0)] + [swap(columns_of(array, by), by) for by in range(1, groups)],
            axis=0,
        )

    def block_of(array, by):
        at = lax.rem(rank + by + ranks, ranks) * rows
        return lax.dynamic_slice_in_dim(array, at, rows, axis=0)

    cos, sin, visible = position_tables(document_ids, HD)
    inverse, unit_rows, normed_shard = normalize(section_inputs[0], gain)
    normed = lax.all_gather(normed_shard, "tensor", axis=0, tiled=True)
    query = jnp.dot(normed, w_query, preferred_element_type=jnp.float32)
    keys = jnp.dot(normed, w_key, preferred_element_type=jnp.float32)
    values = jnp.dot(normed, w_value, preferred_element_type=jnp.float32)
    query_rot, key_rot, value_low, prob_low, mixed = attention_forward(
        query, keys, values, cos, sin, visible
    )
    normed_all = every_sequence_part(normed)
    mixed_all = every_sequence(
        jnp.concatenate([block_of(mixed, -by) for by in range(ranks)], axis=0)
    )

    saved_input = None
    saved_cot = None
    saved_grads = None
    result = None
    for turn in range(pipes):
        home = last - turn
        active = section == home
        if turn == 0:
            blocks = [upstream_grad] + [
                relay(upstream_grad, home, home, by) for by in range(1, ranks)
            ]
        else:
            blocks = [relay(result, home + 1, home, by) for by in range(ranks)]
        incoming = blocks[0]
        cotangent = jnp.concatenate(blocks, axis=0)
        grad_mixed = dot_nt(cotangent, w_output).astype(jnp.bfloat16)
        grad_mixed = jnp.concatenate(
            [
                lax.dynamic_slice_in_dim(
                    grad_mixed, lax.rem(rank - b + ranks, ranks) * rows, rows, axis=0
                )
                for b in range(ranks)
            ],
            axis=0,
        )
        grads = attention_backward(grad_mixed, query_rot, key_rot, value_low, prob_low, cos, sin)

        def term(by):
            return (
                dot_nt(block_of(grads[0], by), w_query)
                + dot_nt(block_of(grads[1], by), w_key)
                + dot_nt(block_of(grads[2], by), w_value)
            ).astype(jnp.bfloat16)

        arrived = [relay(term(by), home, home, by) for by in range(1, ranks)]
        total = term(0).astype(jnp.float32)
        for one in arrived:
            total = total + one.astype(jnp.float32)
        result = back_norm(total, unit_rows, inverse, gain, incoming)
        if turn == 0:
            saved_input, saved_cot, saved_grads = result, cotangent, grads
        else:
            saved_input = jnp.where(active, result, saved_input)
            saved_cot = jnp.where(active, cotangent, saved_cot)
            saved_grads = [jnp.where(active, new, old) for new, old in zip(grads, saved_grads)]

    scale_out = 1.0 / math.sqrt(groups * seq_len)
    cot_all = every_sequence_part(saved_cot)
    output_grads = dot_tn(mixed_all, cot_all) * scale_out
    query_grads, key_grads, value_grads = [
        dot_tn(normed_all, every_sequence(one)) * scale_out for one in saved_grads
    ]
    return (
        saved_input[None],
        query_grads[None],
        key_grads[None],
        value_grads[None],
        output_grads[None],
    )


def solution(mesh):
    placed = (
        P("pipe", ("dp", "tensor"), None),
        P("pipe", None),
        P("pipe", None, "tensor"),
        P("pipe", None, "tensor"),
        P("pipe", None, "tensor"),
        P("pipe", "tensor", None),
        P(("dp", "tensor"), None),
        P("dp", None),
    )
    return jax.shard_map(
        local,
        mesh=mesh,
        in_specs=placed,
        out_specs=(
            P("pipe", ("dp", "tensor"), None),
            P("pipe", "dp", "tensor"),
            P("pipe", "dp", "tensor"),
            P("pipe", "dp", "tensor"),
            P("pipe", "tensor", "dp"),
        ),
        check_vma=False,
    )
```

```python
import functools
import math

import jax
import jax.numpy as jnp
from jax import lax
from jax.experimental import pallas as pl
from jax.experimental.pallas import tpu as pltpu
from jax.sharding import PartitionSpec as P

HD = 128

epsilon = 1e-05
rope_base = 500000.0


def position_tables(document_ids, head_dim):
    ids = document_ids[0]
    index = jnp.arange(ids.shape[0], dtype=jnp.int32)
    earlier = (ids[None, :] < ids[:, None]).astype(jnp.int32)
    position = index - jnp.sum(earlier, axis=1)
    half = head_dim // 2
    expo = jnp.arange(half, dtype=jnp.float32) * (2.0 / head_dim)
    freq = jnp.exp(expo * -math.log(rope_base))
    angle = position.astype(jnp.float32)[:, None] * freq
    cos, sin = jnp.cos(angle), jnp.sin(angle)
    same = ids[:, None] == ids[None, :]
    visible = jnp.logical_and(same, index[:, None] >= index[None, :])
    return (
        jnp.concatenate([cos, cos], axis=1),
        jnp.concatenate([-sin, sin], axis=1),
        visible.astype(jnp.float32),
    )


def normalize(rows, gain):
    values = rows.astype(jnp.float32)
    inverse = lax.rsqrt(jnp.mean(values * values, axis=-1, keepdims=True) + epsilon)
    unit_rows = values * inverse
    normed = (unit_rows * gain.astype(jnp.float32)).astype(jnp.bfloat16)
    return (inverse, unit_rows, normed)


def back_norm(grad_normed, unit_rows, inverse, gain, incoming):
    grad_unit = grad_normed * gain.astype(jnp.float32)
    branch = (
        grad_unit - unit_rows * jnp.mean(grad_unit * unit_rows, axis=-1, keepdims=True)
    ) * inverse
    return (incoming.astype(jnp.float32) + branch).astype(jnp.bfloat16)


def dot_nt(left, right):
    return lax.dot_general(
        left, right, (((1,), (1,)), ((), ())), preferred_element_type=jnp.float32
    )


def dot_tn(left, right):
    return lax.dot_general(
        left, right, (((0,), (0,)), ((), ())), preferred_element_type=jnp.float32
    )


def forward_kernel(group, q_ref, k_ref, v_ref, cos_ref, sin_ref, vis_ref,
                   qr_ref, kr_ref, vl_ref, prob_ref, mixed_ref):
    def turned(vector):
        return vector * cos_ref[...] + pltpu.roll(vector, HD // 2, 1) * sin_ref[...]

    @pl.when(lax.rem(pl.program_id(0), group) == 0)
    def _():
        kr_ref[...] = turned(k_ref[...]).astype(jnp.bfloat16)
        vl_ref[...] = v_ref[...].astype(jnp.bfloat16)

    query = turned(q_ref[...]).astype(jnp.bfloat16)
    qr_ref[...] = query
    scores = dot_nt(query, kr_ref[...]) * (1.0 / math.sqrt(HD))
    expo = jnp.where(vis_ref[...] > 0.0, jnp.exp(scores), 0.0)
    prob = (expo / jnp.sum(expo, axis=-1, keepdims=True)).astype(jnp.bfloat16)
    prob_ref[0] = prob
    mixed_ref[...] = jnp.dot(prob, vl_ref[...], preferred_element_type=jnp.float32).astype(
        jnp.bfloat16
    )


def attention_forward(query, keys, values, cos, sin, visible):
    seq, q_width = query.shape
    k_width = keys.shape[1]
    heads, group = q_width // HD, q_width // k_width
    per_head = pl.BlockSpec((seq, HD), lambda h: (0, h))
    per_kv = pl.BlockSpec((seq, HD), lambda h: (0, h // group))
    table = pl.BlockSpec((seq, HD), lambda h: (0, 0))
    square = pl.BlockSpec((seq, seq), lambda h: (0, 0))
    return pl.pallas_call(
        functools.partial(forward_kernel, group),
        grid=(heads,),
        in_specs=[per_head, per_kv, per_kv, table, table, square],
        out_specs=[
            per_head,
            per_kv,
            per_kv,
            pl.BlockSpec((1, seq, seq), lambda h: (h, 0, 0)),
            per_head,
        ],
        out_shape=[
            jax.ShapeDtypeStruct((seq, q_width), jnp.bfloat16),
            jax.ShapeDtypeStruct((seq, k_width), jnp.bfloat16),
            jax.ShapeDtypeStruct((seq, k_width), jnp.bfloat16),
            jax.ShapeDtypeStruct((heads, seq, seq), jnp.bfloat16),
            jax.ShapeDtypeStruct((seq, q_width), jnp.bfloat16),
        ],
        compiler_params=pltpu.CompilerParams(vmem_limit_bytes=32 * 1024 * 1024),
        cost_estimate=pl.CostEstimate(
            flops=4 * heads * seq * seq * HD,
            bytes_accessed=2 * heads * seq * seq + 8 * seq * q_width,
            transcendentals=heads * seq * seq,
        ),
    )(query, keys, values, cos, sin, visible)


def backward_kernel(group, gm_ref, q_ref, k_ref, v_ref, prob_ref, cos_ref, sin_ref,
                    gq_ref, gk_ref, gv_ref, key_total, value_total):
    member = lax.rem(pl.program_id(0), group)

    def turned_back(vector):
        return vector * cos_ref[...] - pltpu.roll(vector, HD // 2, 1) * sin_ref[...]

    @pl.when(member == 0)
    def _():
        key_total[...] = jnp.zeros_like(key_total)
        value_total[...] = jnp.zeros_like(value_total)

    grad_mixed = gm_ref[...]
    prob_low = prob_ref[0]
    value_total[...] += dot_tn(prob_low, grad_mixed)
    grad_prob = dot_nt(grad_mixed, v_ref[...])
    prob = prob_low.astype(jnp.float32)
    inner = jnp.sum(grad_prob * prob, axis=-1, keepdims=True)
    score_low = (prob * (grad_prob - inner) * (1.0 / math.sqrt(HD))).astype(jnp.bfloat16)
    gq_ref[...] = turned_back(
        jnp.dot(score_low, k_ref[...], preferred_element_type=jnp.float32)
    ).astype(jnp.bfloat16)
    key_total[...] += dot_tn(score_low, q_ref[...])

    @pl.when(member == group - 1)
    def _():
        gk_ref[...] = turned_back(key_total[...]).astype(jnp.bfloat16)
        gv_ref[...] = value_total[...].astype(jnp.bfloat16)


def attention_backward(grad_mixed, query_rot, key_rot, value_low, prob_low, cos, sin):
    seq, q_width = query_rot.shape
    k_width = key_rot.shape[1]
    heads, group = q_width // HD, q_width // k_width
    per_head = pl.BlockSpec((seq, HD), lambda h: (0, h))
    per_kv = pl.BlockSpec((seq, HD), lambda h: (0, h // group))
    table = pl.BlockSpec((seq, HD), lambda h: (0, 0))
    return pl.pallas_call(
        functools.partial(backward_kernel, group),
        grid=(heads,),
        in_specs=[
            per_head,
            per_head,
            per_kv,
            per_kv,
            pl.BlockSpec((1, seq, seq), lambda h: (h, 0, 0)),
            table,
            table,
        ],
        out_specs=[per_head, per_kv, per_kv],
        out_shape=[
            jax.ShapeDtypeStruct((seq, q_width), jnp.bfloat16),
            jax.ShapeDtypeStruct((seq, k_width), jnp.bfloat16),
            jax.ShapeDtypeStruct((seq, k_width), jnp.bfloat16),
        ],
        scratch_shapes=[pltpu.VMEM((seq, HD), jnp.float32)] * 2,
        compiler_params=pltpu.CompilerParams(vmem_limit_bytes=32 * 1024 * 1024),
        cost_estimate=pl.CostEstimate(
            flops=10 * heads * seq * seq * HD,
            bytes_accessed=2 * heads * seq * seq + 6 * seq * q_width,
            transcendentals=0,
        ),
    )(grad_mixed, query_rot, key_rot, value_low, prob_low, cos, sin)


def local(
    section_inputs,
    norm_gain,
    query_weight,
    key_weight,
    value_weight,
    output_weight,
    upstream_grad,
    document_ids,
):
    pipes = lax.axis_size("pipe")
    groups = lax.axis_size("dp")
    ranks = lax.axis_size("tensor")
    section = lax.axis_index("pipe")
    sequence = lax.axis_index("dp")
    rank = lax.axis_index("tensor")
    width = section_inputs.shape[2]
    seq_len = document_ids.shape[1]
    rows = seq_len // ranks
    part = width // groups
    gain = norm_gain[0]
    w_query, w_key, w_value, w_output = (
        query_weight[0],
        key_weight[0],
        value_weight[0],
        output_weight[0],
    )
    last = pipes - 1
    scale_out = 1.0 / math.sqrt(groups * seq_len)

    def relay(block, source, target, by):
        pairs = [
            (source * ranks + i, target * ranks + (i + by) % ranks) for i in range(ranks)
        ]
        return lax.ppermute(block, ("pipe", "tensor"), pairs)

    def relay_within(block, sections, by):
        pairs = [
            (p * ranks + i, p * ranks + (i + by) % ranks) for p in sections for i in range(ranks)
        ]
        return lax.ppermute(block, ("pipe", "tensor"), pairs)

    def natural(array):
        return jnp.concatenate(
            [
                lax.dynamic_slice_in_dim(
                    array, lax.rem(rank - b + ranks, ranks) * rows, rows, axis=0
                )
                for b in range(ranks)
            ],
            axis=0,
        )

    def swap(block, by):
        return lax.ppermute(block, "dp", [(i, (i + by) % groups) for i in range(groups)])

    def columns_of(array, by):
        at = lax.rem(sequence + by, groups) * part
        return lax.dynamic_slice_in_dim(array, at, part, axis=1)

    def every_sequence(array):
        return jnp.concatenate([array] + [swap(array, by) for by in range(1, groups)], axis=0)

    def every_sequence_part(array):
        return jnp.concatenate(
            [columns_of(array, 0)] + [swap(columns_of(array, by), by) for by in range(1, groups)],
            axis=0,
        )

    def block_of(array, by):
        at = lax.rem(rank + by + ranks, ranks) * rows
        return lax.dynamic_slice_in_dim(array, at, rows, axis=0)

    cos, sin, visible = position_tables(document_ids, HD)
    inverse, unit_rows, normed_shard = normalize(section_inputs[0], gain)
    early = [p for p in range(pipes) if (last - p) % 2 == 0]
    late = [p for p in range(pipes) if (last - p) % 2 == 1]
    first = [relay_within(normed_shard, early, by) for by in range(1, ranks)]
    upstream = [upstream_grad] + [
        relay(upstream_grad, last, last, by) for by in range(1, ranks)
    ]
    seen = sum(one[:8, :128].astype(jnp.float32) for one in first + upstream[1:])
    pairs = [((p + 1) * ranks + i, p * ranks + i) for p in late for i in range(ranks)]
    seen = lax.ppermute(seen, ("pipe", "tensor"), pairs)
    waiting = normed_shard + (seen[0, 0] * 0.0).astype(jnp.bfloat16)
    second = [relay_within(waiting, late, by) for by in range(1, ranks)]
    is_early = lax.rem(last - section, 2) == 0
    held = jnp.concatenate(
        [normed_shard] + [jnp.where(is_early, x, y) for x, y in zip(first, second)], axis=0
    )
    query = natural(jnp.dot(held, w_query, preferred_element_type=jnp.float32))
    keys = natural(jnp.dot(held, w_key, preferred_element_type=jnp.float32))
    values = natural(jnp.dot(held, w_value, preferred_element_type=jnp.float32))
    query_rot, key_rot, value_low, prob_low, mixed = attention_forward(
        query, keys, values, cos, sin, visible
    )
    normed_all = every_sequence_part(natural(held))
    mixed_all = every_sequence(
        jnp.concatenate([block_of(mixed, -by) for by in range(ranks)], axis=0)
    )

    for turn in range(pipes):
        home = last - turn
        active = section == home
        if turn == 0:
            blocks = upstream
        else:
            blocks = [relay(result, home + 1, home, by) for by in range(ranks)]
        incoming = blocks[0]
        cotangent = jnp.concatenate(blocks, axis=0)
        grad_mixed = dot_nt(cotangent, w_output).astype(jnp.bfloat16)
        grad_mixed = natural(grad_mixed)
        grads = attention_backward(grad_mixed, query_rot, key_rot, value_low, prob_low, cos, sin)
        if turn == 0:
            saved_cot, saved_grads = cotangent, grads
        else:
            saved_cot = jnp.where(active, cotangent, saved_cot)
            saved_grads = [jnp.where(active, new, old) for new, old in zip(grads, saved_grads)]
        if turn == last:
            cot_all = every_sequence_part(saved_cot)

        def term(by):
            return (
                dot_nt(block_of(grads[0], by), w_query)
                + dot_nt(block_of(grads[1], by), w_key)
                + dot_nt(block_of(grads[2], by), w_value)
            ).astype(jnp.bfloat16)

        sent = [term(by) for by in range(1, ranks)]
        arrived = [relay(one, home, home, by) for by, one in enumerate(sent, 1)]
        own = term(0)
        if turn == last:
            normed_all, mixed_all, sent, own = lax.optimization_barrier(
                (normed_all, mixed_all, sent, own)
            )
            output_grads = dot_tn(mixed_all, cot_all) * scale_out
            query_grads, key_grads, value_grads = [
                dot_tn(normed_all, every_sequence(one)) * scale_out for one in saved_grads
            ]
            own, output_grads, query_grads, key_grads, value_grads = lax.optimization_barrier(
                (own, output_grads, query_grads, key_grads, value_grads)
            )
        total = own.astype(jnp.float32)
        for one in arrived:
            total = total + one.astype(jnp.float32)
        result = back_norm(total, unit_rows, inverse, gain, incoming)
        saved_input = result if turn == 0 else jnp.where(active, result, saved_input)

    return (
        saved_input[None],
        query_grads[None],
        key_grads[None],
        value_grads[None],
        output_grads[None],
    )


def solution(mesh):
    placed = (
        P("pipe", ("dp", "tensor"), None),
        P("pipe", None),
        P("pipe", None, "tensor"),
        P("pipe", None, "tensor"),
        P("pipe", None, "tensor"),
        P("pipe", "tensor", None),
        P(("dp", "tensor"), None),
        P("dp", None),
    )
    return jax.shard_map(
        local,
        mesh=mesh,
        in_specs=placed,
        out_specs=(
            P("pipe", ("dp", "tensor"), None),
            P("pipe", "dp", "tensor"),
            P("pipe", "dp", "tensor"),
            P("pipe", "dp", "tensor"),
            P("pipe", "tensor", "dp"),
        ),
        check_vma=False,
    )
```
